32 devices in a mesh: groups: 2 (over x), owners: 16 (over z, y, core).
Axes of the slice: x: 2, y: 2, z: 4, core: 2. Of those that a mesh axis runs over, the one named last changes fastest.
Arguments:
- embeddings: bfloat16 [32768, 384], P(('groups', 'owners')), parts along dimension 0, may hold values from -400 to 400
- buckets: int32 [32768], P(('groups', 'owners')), parts along dimension 0, may hold values from 0 to 15, as said below
- ranks: int32 [32768], P(('groups', 'owners')), parts along dimension 0, may hold values from 0 to 16383, each once
Outputs:
- highest: float32 [32768], P(('groups', 'owners')), parts along dimension 0
The draws below stay inside these ranges and needn't reach their ends.
There are 2 independent parts, one for each index of `groups`. The reference program is written for one: setup_inputs(seed, part) draws one part's arguments, and reference() takes and returns one part's arrays. A program takes and returns all parts, laid end to end along the dimension named above; each array names one. Nothing has to cross between parts.
Inputs may be any that keep to these rules, and one draw needn't show every extreme that they name: `buckets`: among the documents of one device no value appears more than 128 times; one value, the same on every device, appears exactly 128 times on every device.
All inputs are finite; a program needn't handle non-finite values.
Results may differ from the reference program's by a relative error of at most 0.0015.
Values may be sent and summed in bfloat16 or wider, within the bound.
No kernel may reach another device: no remote copies, remote signals or barrier semaphores. Data moves between devices by JAX's collectives and lax.ppermute only.
A program may use at most 64 MiB of HBM per device.

```python
import math
import jax
import jax.numpy as jnp
from jax import lax

D = 384
ROWS_DEV = 1024
SHARDS = 4
ROWS = 16384
CLUSTERS = 4
N_OWNERS = 16


def draw_embeddings(key, part):
    key = jax.random.fold_in(key, 7)
    base_key, row_key, col_key = jax.random.split(key, 3)
    row_scale = jnp.exp(jax.random.uniform(row_key, (ROWS, 1), jnp.float32, 0.0, math.log(10.0)))
    col_scale = jnp.exp(jax.random.uniform(col_key, (1, D), jnp.float32, 0.0, math.log(10.0)))
    values = jnp.clip(jax.random.normal(base_key, (ROWS, D), jnp.float32), -4.0, 4.0)
    return (values * row_scale * col_scale).astype(jnp.bfloat16)


def draw_buckets(key, part):
    key = jax.random.fold_in(key, 11)
    hot_key, limit_key, order_key = jax.random.split(key, 3)
    capacity = 2 * ROWS_DEV // N_OWNERS
    hot_bucket = jax.random.randint(hot_key, (), 0, N_OWNERS)
    limits = jax.random.randint(limit_key, (N_OWNERS,), capacity // 2, capacity + 1)
    limits = jnp.where(jnp.arange(N_OWNERS) == hot_bucket, capacity, limits)
    slot_ids = jnp.arange(N_OWNERS * capacity)
    owner_of = slot_ids // capacity
    within = slot_ids % capacity
    usable = within < limits[owner_of]

    def one_device(device_key):
        first_key, second_key = jax.random.split(device_key)
        shuffle = jax.random.permutation(first_key, N_OWNERS * capacity)
        scores = jnp.where(owner_of == hot_bucket, 0, jnp.where(usable, 1 + shuffle, 2 + N_OWNERS * capacity + shuffle))
        chosen = jnp.argsort(scores, stable=True)[:ROWS_DEV]
        picked = owner_of[chosen]
        return jax.random.permutation(second_key, picked)
    device_keys = jax.random.split(order_key, N_OWNERS)
    return jax.vmap(one_device)(device_keys).reshape(-1).astype(jnp.int32)


def setup_inputs(seed: int = 0, part: int = 0) -> dict:
    key_list = jax.random.split(jax.random.key(seed), 4)
    part_splits = jax.random.split(jax.random.fold_in(key_list[3], part), 4)
    return {
        "embeddings": draw_embeddings(jax.random.fold_in(jax.random.fold_in(key_list[3], part), 71), part),
        "buckets": draw_buckets(jax.random.fold_in(jax.random.fold_in(key_list[3], part), 71), part),
        "ranks": jax.random.permutation(part_splits[2], ROWS).astype(jnp.int32),
    }


far_rank = 1073741824

def normalize(rows_in):
    widened = rows_in.astype(jnp.float32)
    total = lax.optimization_barrier(jnp.sum(widened * widened, axis=-1, keepdims=True)) + 1e-06
    factor = lax.rsqrt(total)
    return (widened * factor).astype(jnp.bfloat16)

def reference(embeddings, buckets, ranks):
    unit_rows = normalize(embeddings)
    cluster = (buckets // SHARDS).astype(jnp.int32)
    sorting = jnp.argsort(cluster, stable=True).astype(jnp.int32)
    widest = 8 * ROWS_DEV
    labels = jnp.arange(CLUSTERS, dtype=jnp.int32)
    cluster_sizes = lax.optimization_barrier(jnp.sum((cluster[None, :] == labels[:, None]).astype(jnp.int32), axis=1)).astype(jnp.int32)
    cluster_starts = (jnp.cumsum(cluster_sizes) - cluster_sizes).astype(jnp.int32)
    sorted_unit = jnp.concatenate([unit_rows[sorting], jnp.zeros((widest, D), jnp.bfloat16)], axis=0)
    sorted_rank = jnp.concatenate([ranks[sorting], jnp.full((widest,), far_rank, jnp.int32)], axis=0)

    def one_cluster(cluster_index):
        first_row = cluster_starts[cluster_index].astype(jnp.int32)
        live_rows = cluster_sizes[cluster_index]
        columns = lax.dynamic_slice_in_dim(sorted_unit, first_row, widest, 0)
        column_rank = lax.dynamic_slice_in_dim(sorted_rank, first_row, widest, 0)
        column_rank = jnp.where(jnp.arange(widest) < live_rows, column_rank, far_rank)
        query_tiles = columns.reshape(widest // 512, 512, D)
        query_ranks = column_rank.reshape(widest // 512, 512)

        def one_tile(packed):
            tile_rows, tile_rank = packed
            scores = jnp.dot(tile_rows, columns.T, preferred_element_type=jnp.float32)
            scores = jnp.where(column_rank[None, :] < tile_rank[:, None], scores, -1.0)
            return lax.optimization_barrier(jnp.max(scores, axis=1))
        return lax.map(one_tile, (query_tiles, query_ranks)).reshape(widest)
    per_cluster = lax.map(one_cluster, labels)
    sorted_cluster = cluster[sorting]
    offset = jnp.arange(ROWS, dtype=jnp.int32) - cluster_starts[sorted_cluster]
    best_sorted = per_cluster[sorted_cluster, offset]
    return jnp.zeros((ROWS,), jnp.float32).at[sorting].set(best_sorted)
```

```python
import functools

import jax
import jax.numpy as jnp
from jax import lax
from jax.experimental import pallas as pl
from jax.experimental.pallas import tpu as pltpu
from jax.sharding import PartitionSpec as P

far_rank = 1073741824
SHARDS = 4
EXTRA = 16
PAD_RANK = 65536.0
VMEM_LIMIT = 48 * 1024 * 1024


def from_partner(value, axis, mask):
    pairs = [(source, source ^ mask) for source in range(lax.axis_size(axis))]
    return lax.ppermute(value, axis, pairs)


def dot_nt(left, right):
    return lax.dot_general(left, right, (((1,), (1,)), ((), ())), preferred_element_type=jnp.float32)


def one_hot(keys, first, count):
    rows = lax.broadcasted_iota(jnp.int32, (count, keys.shape[1]), 0) + first
    return jnp.where(rows == keys, 1.0, 0.0).astype(jnp.bfloat16)


def route_kernel(chunks, docs, tile, home_ref, rows_ref, bucket_ref, rank_ref, *out_refs):
    row_count, width = rows_ref.shape
    home = home_ref[0]
    distance = (bucket_ref[...] // SHARDS) ^ home
    lines = max(chunks, 16)
    member = lax.broadcasted_iota(jnp.int32, (lines, row_count), 0) == distance
    member_f = jnp.where(member, 1.0, 0.0)
    earlier = (
        lax.broadcasted_iota(jnp.int32, (row_count, row_count), 0)
        < lax.broadcasted_iota(jnp.int32, (row_count, row_count), 1)
    )
    before = jnp.dot(
        member_f.astype(jnp.bfloat16),
        jnp.where(earlier, 1.0, 0.0).astype(jnp.bfloat16),
        preferred_element_type=jnp.float32,
    )
    place = jnp.sum(before * member_f, axis=0, keepdims=True)
    over = jnp.where(jnp.max(place, axis=1, keepdims=True) >= docs, 1.0, 0.0)
    keys = jnp.where(place < docs, distance * tile + place.astype(jnp.int32), -1)
    out_refs[chunks][...] = keys
    widened = rows_ref[...].astype(jnp.float32)
    total = jnp.sum(widened * widened, axis=1, keepdims=True) + 1e-06
    unit = (widened * lax.rsqrt(total)).astype(jnp.bfloat16)
    ranks = rank_ref[...]
    digit = lax.broadcasted_iota(jnp.int32, (EXTRA, row_count), 0)
    high = (ranks // 256 - 256).astype(jnp.float32)
    low = (ranks % 256).astype(jnp.float32)
    digits = jnp.where(digit == 0, high, jnp.where(digit == 1, low, 0.0)).astype(jnp.bfloat16)
    for chunk in range(chunks):
        chosen = one_hot(keys, chunk * tile, tile)
        moved = jnp.dot(chosen, unit, preferred_element_type=jnp.float32)
        out_refs[chunk][...] = moved.astype(jnp.bfloat16)
        tail = dot_nt(digits, chosen)
        tail = jnp.where(lax.broadcasted_iota(jnp.int32, (EXTRA, tile), 0) == 2, over, tail)
        if tile < width:
            tail = jnp.concatenate([tail, jnp.zeros((EXTRA, width - tile), jnp.float32)], axis=1)
        out_refs[chunk][docs:tile, :] = tail.astype(jnp.bfloat16)


def route(chunks, docs, tile, embeddings, buckets, ranks, home):
    row_count, width = embeddings.shape
    smem = pl.BlockSpec(memory_space=pltpu.SMEM)
    vmem = pl.BlockSpec(memory_space=pltpu.VMEM)
    return pl.pallas_call(
        functools.partial(route_kernel, chunks, docs, tile),
        out_shape=[jax.ShapeDtypeStruct((tile, width), jnp.bfloat16)] * chunks
        + [jax.ShapeDtypeStruct((1, row_count), jnp.int32)],
        in_specs=[smem, vmem, vmem, vmem],
        out_specs=[vmem] * (chunks + 1),
        compiler_params=pltpu.CompilerParams(vmem_limit_bytes=VMEM_LIMIT),
        cost_estimate=pl.CostEstimate(
            flops=2 * chunks * tile * row_count * width, bytes_accessed=4 * row_count * width, transcendentals=0
        ),
        name="route",
    )(home, embeddings, buckets.reshape(1, row_count), ranks.reshape(1, row_count))


def rank_row(chunk_ref, docs, tile):
    tail = chunk_ref[docs:tile, :].astype(jnp.float32)
    return tail[0:1, :tile] * 256.0 + tail[1:2, :tile] + PAD_RANK


def spread_ranks(chunk_ref, docs, tile, target_ref, first):
    tail = chunk_ref[docs:tile, :].astype(jnp.float32)
    same = lax.broadcasted_iota(jnp.int32, (128, 128), 0) == lax.broadcasted_iota(jnp.int32, (128, 128), 1)
    ones = jnp.ones((256, 128), jnp.bfloat16)
    for block in range(tile // 128):
        lanes = slice(128 * block, 128 * block + 128)
        diagonal = jnp.concatenate(
            [jnp.where(same, tail[0:1, lanes] * 256.0, 0.0), jnp.where(same, tail[1:2, lanes], 0.0)], axis=1
        ).astype(jnp.bfloat16)
        spread = jnp.dot(diagonal, ones, preferred_element_type=jnp.float32) + PAD_RANK
        target_ref[first + 128 * block : first + 128 * block + 128, :] = spread


def fold(best, query, query_rank, column_ref, column_rank):
    scores = dot_nt(column_ref[...], query)
    lanes = query.shape[0]
    column_rank = jnp.concatenate([column_rank] * (lanes // 128), axis=1)
    scores = jnp.where(column_rank < query_rank, scores, -1.0)
    return jnp.maximum(best, jnp.max(scores.reshape(-1, 8, lanes), axis=0))


def compare_kernel(docs, tile, query_count, column_count, *refs):
    query_refs = refs[:query_count]
    column_refs = refs[query_count : query_count + column_count]
    out_refs = refs[query_count + column_count : 2 * query_count + column_count]
    over_ref, spread_ref, query_ref, query_rank_ref, best_ref = refs[2 * query_count + column_count :]
    over = jnp.zeros((1, 128), jnp.float32)
    for column in column_refs:
        over = jnp.maximum(over, column[docs:tile, :].astype(jnp.float32)[2:3, :128])
    over_ref[...] = over.astype(jnp.int32)
    for place, column in enumerate(column_refs):
        spread_ranks(column, docs, tile, spread_ref, place * tile)
    for place, query in enumerate(query_refs):
        query_ref[place * tile : place * tile + tile, :] = query[...]
        query_rank_ref[:, place * tile : place * tile + tile] = rank_row(query, docs, tile)
    lanes = 256

    def one_tile(step, carry):
        first = pl.multiple_of(step * lanes, lanes)
        query = query_ref[pl.ds(first, lanes), :]
        query_rank = query_rank_ref[:, pl.ds(first, lanes)]
        best = jnp.full((8, lanes), -1.0, jnp.float32)
        for place, column in enumerate(column_refs):
            best = fold(best, query, query_rank, column, spread_ref[place * tile : place * tile + tile, :])
        best_ref[:, pl.ds(first, lanes)] = jnp.max(best, axis=0, keepdims=True)
        return carry

    lax.fori_loop(0, query_count * tile // lanes, one_tile, 0)
    for place, out in enumerate(out_refs):
        out[...] = best_ref[:, place * tile : place * tile + tile]


def compare(docs, tile, queries, columns):
    vmem = pl.BlockSpec(memory_space=pltpu.VMEM)
    query_count, column_count = len(queries), len(columns)
    width = queries[0].shape[1]
    return pl.pallas_call(
        functools.partial(compare_kernel, docs, tile, query_count, column_count),
        out_shape=[jax.ShapeDtypeStruct((1, tile), jnp.float32)] * query_count
        + [jax.ShapeDtypeStruct((1, 128), jnp.int32)],
        in_specs=[vmem] * (query_count + column_count),
        out_specs=[vmem] * (query_count + 1),
        scratch_shapes=[
            pltpu.VMEM((column_count * tile, 128), jnp.float32),
            pltpu.VMEM((query_count * tile, width), jnp.bfloat16),
            pltpu.VMEM((1, query_count * tile), jnp.float32),
            pltpu.VMEM((1, query_count * tile), jnp.float32),
        ],
        compiler_params=pltpu.CompilerParams(vmem_limit_bytes=VMEM_LIMIT),
        cost_estimate=pl.CostEstimate(
            flops=2 * query_count * column_count * tile * tile * width,
            bytes_accessed=2 * (query_count + column_count) * tile * width,
            transcendentals=0,
        ),
        name="compare",
    )(*queries, *columns)


def place_kernel(chunks, tile, key_ref, *refs):
    keys = key_ref[...]
    out_ref = refs[chunks]
    gathered = jnp.zeros((16, keys.shape[1]), jnp.float32)
    line = lax.broadcasted_iota(jnp.int32, (16, tile), 0)
    for chunk in range(chunks):
        value = refs[chunk][...]
        first = value.astype(jnp.bfloat16).astype(jnp.float32)
        second = (value - first).astype(jnp.bfloat16).astype(jnp.float32)
        third = value - first - second
        parts = jnp.where(line == 0, first, jnp.where(line == 1, second, jnp.where(line == 2, third, 0.0)))
        gathered += jnp.dot(
            parts.astype(jnp.bfloat16), one_hot(keys, chunk * tile, tile), preferred_element_type=jnp.float32
        )
    out_ref[...] = jnp.sum(gathered, axis=0, keepdims=True)


def place(chunks, tile, keys, values):
    vmem = pl.BlockSpec(memory_space=pltpu.VMEM)
    return pl.pallas_call(
        functools.partial(place_kernel, chunks, tile),
        out_shape=jax.ShapeDtypeStruct(keys.shape, jnp.float32),
        in_specs=[vmem] * (chunks + 1),
        out_specs=vmem,
        compiler_params=pltpu.CompilerParams(vmem_limit_bytes=VMEM_LIMIT),
        name="place",
    )(keys, *values)


def normalize(rows_in):
    widened = rows_in.astype(jnp.float32)
    total = jnp.sum(widened * widened, axis=-1, keepdims=True) + 1e-06
    factor = lax.rsqrt(total)
    return (widened * factor).astype(jnp.bfloat16)


def fold_block(highest, queries, query_rank, columns, column_rank):
    query_count = queries.shape[0]
    tile_rows = min(512, query_count)
    pieces = query_count // tile_rows
    query_tiles = queries.reshape(pieces, tile_rows, queries.shape[1])
    rank_tiles = query_rank.reshape(pieces, tile_rows)
    best_tiles = highest.reshape(pieces, tile_rows)

    def one_query_tile(packed):
        tile_queries, tile_rank, running = packed
        scores = lax.dot_general(
            tile_queries, columns, (((1,), (1,)), ((), ())), preferred_element_type=jnp.float32
        )
        scores = jnp.where(column_rank[None, :] < tile_rank[:, None], scores, -1.0)
        return jnp.maximum(running, jnp.max(scores, axis=1))

    return lax.map(one_query_tile, (query_tiles, rank_tiles, best_tiles)).reshape(query_count)


def roomy(embeddings, buckets, ranks):
    owner_count = lax.axis_size("owners")
    row_count, feature_width = embeddings.shape
    capacity = 2 * row_count // owner_count
    slot_total = owner_count * capacity
    targets = jnp.arange(owner_count, dtype=jnp.int32)
    onehot = (buckets[:, None] == targets[None, :]).astype(jnp.int32)
    before = jnp.cumsum(onehot, axis=0) - onehot
    slot_index = jnp.sum(before * onehot, axis=1)
    position = buckets * capacity + slot_index
    source = (
        jnp.full((slot_total,), row_count, jnp.int32)
        .at[position]
        .set(jnp.arange(row_count, dtype=jnp.int32))
    )
    padded_rows = jnp.concatenate([embeddings, jnp.zeros((1, feature_width), jnp.bfloat16)], axis=0)
    padded_rank = jnp.concatenate([ranks, jnp.full((1,), far_rank, jnp.int32)], axis=0)
    send_rows = padded_rows[source]
    send_rank = padded_rank[source]
    got_rows, got_rank = (
        lax.all_to_all(
            send_rows.reshape(owner_count, capacity, feature_width),
            "owners",
            split_axis=0,
            concat_axis=0,
            tiled=True,
        ),
        lax.all_to_all(
            send_rank.reshape(owner_count, capacity),
            "owners",
            split_axis=0,
            concat_axis=0,
            tiled=True,
        ),
    )
    got_rows = got_rows.reshape(slot_total, feature_width)
    got_rank = got_rank.reshape(slot_total)
    unit_rows = normalize(got_rows)
    own_block = (unit_rows, got_rank)
    highest = jnp.full((slot_total,), -1.0, jnp.float32)
    highest = fold_block(highest, unit_rows, got_rank, unit_rows, got_rank)
    near_block = from_partner((own_block[0], own_block[1]), "owners", 0)
    across_block = from_partner((own_block[0], own_block[1]), "owners", 1)
    diagonal_block = from_partner((across_block[0], across_block[1]), "owners", 0)
    highest = fold_block(highest, unit_rows, got_rank, near_block[0], near_block[1])
    highest = fold_block(highest, unit_rows, got_rank, across_block[0], across_block[1])
    highest = fold_block(highest, unit_rows, got_rank, diagonal_block[0], diagonal_block[1])
    returned = lax.all_to_all(
        highest.reshape(owner_count, capacity), "owners", split_axis=0, concat_axis=0, tiled=True
    )
    return returned.reshape(slot_total)[position]


def body(embeddings, buckets, ranks):
    owner_count = lax.axis_size("owners")
    row_count, _ = embeddings.shape
    chunks = owner_count // SHARDS
    full = SHARDS * 2 * row_count // owner_count
    tile = -(-(3 * full // 4) // 128) * 128
    docs = tile - EXTRA
    home = (lax.axis_index("owners") // SHARDS).astype(jnp.int32).reshape(1)
    *sent, keys = route(chunks, docs, tile, embeddings, buckets, ranks, home)
    own = [sent[0]] + [from_partner(sent[k], "owners", SHARDS * k) for k in range(1, chunks)]
    across = [from_partner(block, "owners", 2) for block in own]
    near = [from_partner(block, "owners", 1) for block in own]
    diagonal = [from_partner(block, "owners", 1) for block in across]
    columns = own + near + across + diagonal
    *best, over = compare(docs, tile, own, columns)
    returned = [best[0]] + [from_partner(best[k], "owners", SHARDS * k) for k in range(1, chunks)]
    found = place(chunks, tile, keys, returned).reshape(row_count)
    return lax.cond(over[0, 0] > 0, roomy, lambda *_: found, embeddings, buckets, ranks)


def solution(mesh):
    in_specs = (P(("groups", "owners"), None), P(("groups", "owners")), P(("groups", "owners")))
    out_specs = P(("groups", "owners"))
    return jax.shard_map(body, mesh=mesh, in_specs=in_specs, out_specs=out_specs, check_vma=False)
```

```python
import functools

import jax
import jax.numpy as jnp
from jax import lax
from jax.experimental import pallas as pl
from jax.experimental.pallas import tpu as pltpu
from jax.sharding import PartitionSpec as P

SHARDS = 4
EXTRA = 16
PAD_RANK = 65536.0
LANES = 512
VMEM_LIMIT = 48 * 1024 * 1024
ROUTE_VMEM_LIMIT = 60 * 1024 * 1024


def from_partner(value, axis, mask):
    pairs = [(source, source ^ mask) for source in range(lax.axis_size(axis))]
    return lax.ppermute(value, axis, pairs)


def dot_nt(left, right):
    return lax.dot_general(left, right, (((1,), (1,)), ((), ())), preferred_element_type=jnp.float32)


def one_hot(keys, first, count):
    rows = lax.broadcasted_iota(jnp.int32, (count, keys.shape[1]), 0) + first
    return jnp.where(rows == keys, 1.0, 0.0).astype(jnp.bfloat16)


def lead(tile, width):
    return 2 * -(-tile // width) + 1


def fold_lines(lines, over, width):
    tile = lines.shape[1]
    rows = []
    for line in range(2):
        for first in range(0, tile, width):
            row = lines[line : line + 1, first : min(first + width, tile)]
            if row.shape[1] < width:
                row = jnp.concatenate([row, jnp.zeros((1, width - row.shape[1]), jnp.float32)], axis=1)
            rows.append(row)
    rows.append(jnp.broadcast_to(over, (1, width)))
    rows.append(jnp.zeros((EXTRA - len(rows), width), jnp.float32))
    return jnp.concatenate(rows, axis=0)


def rank_lines(head_ref, tile):
    width = head_ref.shape[1]
    tail = head_ref[0:EXTRA, :].astype(jnp.float32)
    pieces = -(-tile // width)
    lines = [
        jnp.concatenate([tail[pieces * line + p : pieces * line + p + 1] for p in range(pieces)], axis=1)[:, :tile]
        for line in range(2)
    ]
    return lines[0], lines[1], tail[2 * pieces : 2 * pieces + 1, :128]


def route_kernel(cuts, home_ref, rows_hbm_ref, bucket_hbm_ref, rank_hbm_ref, *refs):
    *out_refs, rows_ref, bucket_ref, rank_ref, copied = refs
    sources = (bucket_hbm_ref, rank_hbm_ref, rows_hbm_ref)
    targets = (bucket_ref, rank_ref, rows_ref)
    copies = [pltpu.make_async_copy(*pair, copied.at[place]) for place, pair in enumerate(zip(sources, targets))]
    for copy in copies:
        copy.start()
    row_count, width = rows_ref.shape
    chunks, tile = len(cuts), sum(cuts[0])
    used = lead(tile, width)
    copies[0].wait()
    distance = (bucket_ref[...] // SHARDS) ^ home_ref[0]
    lines, span = max(chunks, 16), 256
    earlier = lax.broadcasted_iota(jnp.int32, (span, span), 0) < lax.broadcasted_iota(jnp.int32, (span, span), 1)
    earlier = jnp.where(earlier, 1.0, 0.0).astype(jnp.bfloat16)
    member = lax.broadcasted_iota(jnp.int32, (lines, row_count), 0) == distance
    member = jnp.where(member, 1.0, 0.0)
    past, places = jnp.zeros((lines, 1), jnp.float32), []
    for first in range(0, row_count, span):
        some = member[:, first : first + span]
        before = jnp.dot(some.astype(jnp.bfloat16), earlier, preferred_element_type=jnp.float32) + past
        places.append(jnp.sum(before * some, axis=0, keepdims=True))
        past += jnp.sum(some, axis=1, keepdims=True)
    place = jnp.concatenate(places, axis=1)
    over = jnp.where(jnp.max(past, axis=0, keepdims=True) > tile - used, 1.0, 0.0)
    keys = jnp.where(place < tile - used, distance * tile + place.astype(jnp.int32) + used, -1)
    out_refs[-1][...] = keys
    copies[1].wait()
    ranks = rank_ref[...]
    digit = lax.broadcasted_iota(jnp.int32, (EXTRA, row_count), 0)
    high = (ranks // 256 - 256).astype(jnp.float32)
    low = (ranks % 256).astype(jnp.float32)
    digits = jnp.where(digit == 0, high, jnp.where(digit == 1, low, 0.0)).astype(jnp.bfloat16)
    copies[2].wait()
    widened = rows_ref[...].astype(jnp.float32)
    total = jnp.sum(widened * widened, axis=1, keepdims=True) + 1e-06
    unit = (widened * lax.rsqrt(total)).astype(jnp.bfloat16)
    turned = jnp.transpose(digits.astype(jnp.float32)).astype(jnp.bfloat16)
    turned = jnp.concatenate([turned, jnp.zeros((row_count, 128 - EXTRA), jnp.bfloat16)], axis=1)
    unit = jnp.concatenate([unit, turned], axis=1)
    pieces = iter(out_refs)
    for chunk in range(chunks):
        chosen = one_hot(keys, chunk * tile, tile)
        both = jnp.dot(chosen, unit, preferred_element_type=jnp.float32)
        moved = both[:, :width].astype(jnp.bfloat16)
        first = 0
        for rows in cuts[chunk]:
            piece = next(pieces)
            piece[...] = moved[first : first + rows, :]
            if first == 0:
                tail = fold_lines(jnp.transpose(both[:, width:])[:EXTRA], over, width).astype(jnp.bfloat16)
                is_lead = lax.broadcasted_iota(jnp.int32, (EXTRA, width), 0) < used
                piece[0:EXTRA, :] = jnp.where(is_lead, tail, moved[0:EXTRA, :])
            first += rows


def route(cuts, embeddings, buckets, ranks, home):
    row_count, width = embeddings.shape
    smem = pl.BlockSpec(memory_space=pltpu.SMEM)
    vmem = pl.BlockSpec(memory_space=pltpu.VMEM)
    shapes = [jax.ShapeDtypeStruct((rows, width), jnp.bfloat16) for cut in cuts for rows in cut]
    *pieces, keys = pl.pallas_call(
        functools.partial(route_kernel, cuts),
        out_shape=shapes + [jax.ShapeDtypeStruct((1, row_count), jnp.int32)],
        in_specs=[smem] + [pl.BlockSpec(memory_space=pl.ANY)] * 3,
        out_specs=[vmem] * (len(shapes) + 1),
        scratch_shapes=[
            pltpu.VMEM((row_count, width), jnp.bfloat16),
            pltpu.VMEM((1, row_count), jnp.int32),
            pltpu.VMEM((1, row_count), jnp.int32),
            pltpu.SemaphoreType.DMA((3,)),
        ],
        compiler_params=pltpu.CompilerParams(vmem_limit_bytes=ROUTE_VMEM_LIMIT),
        name="route",
    )(home, embeddings, buckets.reshape(1, row_count), ranks.reshape(1, row_count))
    pieces = iter(pieces)
    return [[next(pieces) for _ in cut] for cut in cuts], keys


def spread_ranks(head_ref, tile, offset, target_ref, first, rows):
    high, low, _ = rank_lines(head_ref, tile)
    same = lax.broadcasted_iota(jnp.int32, (128, 128), 0) == lax.broadcasted_iota(jnp.int32, (128, 128), 1)
    ones = jnp.ones((256, 128), jnp.bfloat16)
    for block in range(0, rows, 128):
        lanes = slice(offset + block, offset + block + 128)
        diagonal = jnp.concatenate(
            [jnp.where(same, high[:, lanes] * 256.0, 0.0), jnp.where(same, low[:, lanes], 0.0)], axis=1
        ).astype(jnp.bfloat16)
        spread = jnp.dot(diagonal, ones, preferred_element_type=jnp.float32) + PAD_RANK
        target_ref[first + block : first + block + 128, :] = spread


def fold(best, query, query_rank, column_ref, column_rank):
    scores = dot_nt(column_ref[...], query)
    lanes = query.shape[0]
    column_rank = jnp.concatenate([column_rank] * (lanes // 128), axis=1)
    scores = jnp.where(column_rank < query_rank, scores, -1.0)
    return jnp.maximum(best, jnp.max(scores.reshape(-1, 8, lanes), axis=0))


def compare_kernel(plan, *refs):
    tile, queries, columns, jobs, has_held, has_best, has_over, keep, split, piece_count, lane_count = plan
    refs = iter(refs)
    piece_refs = [next(refs) for _ in range(piece_count)]
    held_refs = [next(refs) for _ in range(2 * has_held)]
    start_ref = next(refs) if has_best else None
    past_ref = next(refs) if has_over else None
    out_refs = [next(refs) for _ in range(lane_count // tile if split else 1)]
    over_ref = next(refs)
    query_ref, query_rank_ref = held_refs if has_held else (next(refs), next(refs))
    spread_ref, best_ref = refs

    over = past_ref[...].astype(jnp.float32) if has_over else jnp.zeros((1, 128), jnp.float32)
    spans, first = [], 0
    for head, piece, offset in columns:
        rows = piece_refs[piece].shape[0]
        if offset == 0:
            over = jnp.maximum(over, rank_lines(piece_refs[head], tile)[2])
        spread_ranks(piece_refs[head], tile, offset, spread_ref, first, rows)
        spans.append((piece_refs[piece], first, first + rows))
        first += rows
    over_ref[...] = over.astype(jnp.int32)

    first = 0
    for query in queries:
        high, low, _ = rank_lines(piece_refs[query[0]], tile)
        query_rank_ref[:, first : first + tile] = high * 256.0 + low + PAD_RANK
        for piece in query:
            rows = piece_refs[piece].shape[0]
            query_ref[first : first + rows, :] = piece_refs[piece][...]
            first += rows
    best_ref[...] = jnp.full((1, lane_count), -1.0, jnp.float32)
    if has_best:
        best_ref[:, : start_ref.shape[1]] = start_ref[...]

    for lane_from, lane_to, column_from, column_to in jobs:

        def one_tile(step, carry, column_from=column_from, column_to=column_to):
            lanes = pl.ds(pl.multiple_of(step * LANES, LANES), LANES)
            query = query_ref[lanes, :]
            query_rank = query_rank_ref[:, lanes]
            best = jnp.broadcast_to(best_ref[:, lanes], (8, LANES))
            for column_ref, start, stop in spans[column_from:column_to]:
                best = fold(best, query, query_rank, column_ref, spread_ref[start:stop, :])
            best_ref[:, lanes] = jnp.max(best, axis=0, keepdims=True)
            return carry

        lax.fori_loop(lane_from // LANES, lane_to // LANES, one_tile, 0)
    if split:
        for place, out_ref in enumerate(out_refs):
            out_ref[...] = best_ref[:, place * tile : place * tile + tile]
    else:
        out_refs[0][...] = best_ref[...]


def columns_of(block):
    first, out = 0, []
    for piece in block:
        out.append((block[0], piece, first))
        first += piece.shape[0]
    return out


def compare(tile, columns, jobs, queries=(), held=(), best=None, over=None, keep=False, split=False):
    pieces = []

    def index_of(array):
        for place, other in enumerate(pieces):
            if other is array:
                return place
        pieces.append(array)
        return len(pieces) - 1

    column_plan = tuple((index_of(head), index_of(piece), offset) for head, piece, offset in columns)
    query_plan = tuple(tuple(index_of(piece) for piece in block) for block in queries)
    lane_count = held[0].shape[0] if held else len(queries) * tile
    width = pieces[0].shape[1]
    plan = (
        tile, query_plan, column_plan, tuple(jobs), bool(held), best is not None, over is not None, keep, split,
        len(pieces), lane_count,
    )
    operands = pieces + list(held) + [array for array in (best, over) if array is not None]
    query_shapes = [((lane_count, width), jnp.bfloat16), ((1, lane_count), jnp.float32)]
    lines = lane_count // tile if split else 1
    outs = [jax.ShapeDtypeStruct((1, lane_count // lines), jnp.float32)] * lines
    outs.append(jax.ShapeDtypeStruct((1, 128), jnp.int32))
    scratch = []
    if keep:
        outs += [jax.ShapeDtypeStruct(*shape) for shape in query_shapes]
    elif not held:
        scratch += [pltpu.VMEM(*shape) for shape in query_shapes]
    column_rows = sum(piece.shape[0] for _, piece, _ in columns)
    scratch += [pltpu.VMEM((column_rows, 128), jnp.float32), pltpu.VMEM((1, lane_count), jnp.float32)]
    vmem = pl.BlockSpec(memory_space=pltpu.VMEM)
    results = pl.pallas_call(
        functools.partial(compare_kernel, plan),
        out_shape=outs,
        in_specs=[vmem] * len(operands),
        out_specs=[vmem] * len(outs),
        scratch_shapes=scratch,
        compiler_params=pltpu.CompilerParams(vmem_limit_bytes=VMEM_LIMIT),
        name="compare",
    )(*operands)
    found = results[:lines] if split else results[0]
    return found, results[lines], results[lines + 1 :]


def place_kernel(chunks, tile, key_ref, *refs):
    keys = key_ref[...]
    out_ref = refs[chunks]
    gathered = jnp.zeros((16, keys.shape[1]), jnp.float32)
    line = lax.broadcasted_iota(jnp.int32, (16, tile), 0)
    for chunk in range(chunks):
        value = refs[chunk][...]
        first = value.astype(jnp.bfloat16).astype(jnp.float32)
        second = (value - first).astype(jnp.bfloat16).astype(jnp.float32)
        third = value - first - second
        parts = jnp.where(line == 0, first, jnp.where(line == 1, second, jnp.where(line == 2, third, 0.0)))
        gathered += jnp.dot(
            parts.astype(jnp.bfloat16), one_hot(keys, chunk * tile, tile), preferred_element_type=jnp.float32
        )
    out_ref[...] = jnp.sum(gathered, axis=0, keepdims=True)


def place(chunks, tile, keys, values):
    vmem = pl.BlockSpec(memory_space=pltpu.VMEM)
    return pl.pallas_call(
        functools.partial(place_kernel, chunks, tile),
        out_shape=jax.ShapeDtypeStruct(keys.shape, jnp.float32),
        in_specs=[vmem] * (chunks + 1),
        out_specs=vmem,
        compiler_params=pltpu.CompilerParams(vmem_limit_bytes=VMEM_LIMIT),
        name="place",
    )(keys, *values)


def swap(block, mask):
    return [from_partner(piece, "owners", mask) for piece in block]


def after(value, *others):
    return lax.optimization_barrier((value, *others))[0]


def give_back(chunks, tile, keys, best):
    returned = [best[0]] + [from_partner(best[k], "owners", SHARDS * k) for k in range(1, chunks)]
    return place(chunks, tile, keys, returned).reshape(keys.shape[1])


def roomy(chunks, tile, embeddings, buckets, ranks, home):
    sent, keys = route(((tile,),) * chunks, embeddings, buckets, ranks, home)
    own = [sent[0]] + [swap(sent[k], SHARDS * k) for k in range(1, chunks)]
    pair = own + [swap(block, 1) for block in own]
    lanes = chunks * tile
    columns = sum(map(columns_of, pair), [])
    best, over, held = compare(tile, columns, ((0, lanes, 0, len(columns)),), own, keep=True)
    columns = sum((columns_of(swap(block, 2)) for block in pair), [])
    best, *_ = compare(tile, columns, ((0, lanes, 0, len(columns)),), held=held, best=best, split=True)
    return give_back(chunks, tile, keys, best)


def snug(chunks, tile, embeddings, buckets, ranks, home):
    sent, keys = route(((tile,),) * chunks, embeddings, buckets, ranks, home)
    lanes, wave = chunks * tile, chunks // 4
    first_lanes = 3 * wave * tile // LANES * LANES
    half_lanes = 2 * wave * tile

    def hop(blocks, mask, *others):
        return [swap([after(piece, *others) for piece in block] if others else block, mask) for block in blocks]

    def z_hop(place, *others):
        group = range(place * wave, place * wave + wave)
        return sum((hop(sent[k : k + 1], SHARDS * k, *others) if k else sent[:1] for k in group), [])

    def columns(*groups):
        return sum(map(columns_of, sum(groups, [])), [])

    z0 = z_hop(0)
    z1 = z_hop(1)
    z2 = z_hop(2)
    z3 = z_hop(3)
    y0 = hop(z0, 2)
    c0 = hop(z0, 1)
    d0 = hop(y0, 1)
    y1 = hop(z1, 2)
    y2 = hop(z2, 2)
    seen = columns(z0, z1, z2, y0, c0, d0)
    k1, over, _ = compare(tile, seen, ((0, first_lanes, 0, len(seen)),), z0 + z1 + z2)
    c1 = hop(z1, 1, k1)
    c2 = hop(z2, 1, k1)
    d1 = hop(y1, 1, k1)
    z3 = [[after(piece, k1) for piece in block] for block in z3]
    y3 = hop(z3, 2)
    c3 = hop(z3, 1)
    d2 = hop(y2, 1)
    every = seen + columns(z3, y2, c3, d2, c1, c2, y1, d1)
    jobs = ((first_lanes, lanes, 0, len(seen)), (0, lanes, len(seen), len(every)))
    k2, over, held = compare(tile, every, jobs, z0 + z1 + z2 + z3, best=k1, over=over, keep=True)
    y3 = [[after(piece, k2) for piece in block] for block in y3]
    d3 = hop(y3, 1)
    last = columns(y3, d3)
    best, over, _ = compare(tile, last, ((0, lanes, 0, len(last)),), held=held, best=k2, over=over, split=True)
    return give_back(chunks, tile, keys, best), over[0, 0] > 0


def body(embeddings, buckets, ranks):
    chunks = lax.axis_size("owners") // SHARDS
    full = SHARDS * 2 * embeddings.shape[0] // lax.axis_size("owners")
    tile = -(-(3 * full // 4) // 128) * 128
    roomy_tile = -(-(full + EXTRA) // 128) * 128
    home = (lax.axis_index("owners") // SHARDS).astype(jnp.int32).reshape(1)
    found, short = snug(chunks, tile, embeddings, buckets, ranks, home)
    return lax.cond(
        short,
        functools.partial(roomy, chunks, roomy_tile),
        lambda *_: found,
        embeddings,
        buckets,
        ranks,
        home,
    )


def solution(mesh):
    in_specs = (P(("groups", "owners"), None), P(("groups", "owners")), P(("groups", "owners")))
    out_specs = P(("groups", "owners"))
    return jax.shard_map(body, mesh=mesh, in_specs=in_specs, out_specs=out_specs, check_vma=False)
```

```python
import functools

import jax
import jax.numpy as jnp
from jax import lax
from jax.experimental import pallas as pl
from jax.experimental.pallas import tpu as pltpu
from jax.sharding import PartitionSpec as P

SHARDS = 4
EXTRA = 16
PAD_RANK = 65536.0
LANES = 512
WHOLE = 5 * 1024 * 1024
VMEM_LIMIT = 48 * 1024 * 1024
ROUTE_VMEM_LIMIT = 60 * 1024 * 1024


def from_partner(value, axis, mask):
    pairs = [(source, source ^ mask) for source in range(lax.axis_size(axis))]
    return lax.ppermute(value, axis, pairs)


def dot_nt(left, right):
    return lax.dot_general(left, right, (((1,), (1,)), ((), ())), preferred_element_type=jnp.float32)


def one_hot(keys, first, count):
    rows = lax.broadcasted_iota(jnp.int32, (count, keys.shape[1]), 0) + first
    return jnp.where(rows == keys, 1.0, 0.0).astype(jnp.bfloat16)


def lead(tile, width):
    return 2 * -(-tile // width) + 1


def fold_lines(lines, over, width):
    tile = lines.shape[1]
    rows = []
    for line in range(2):
        for first in range(0, tile, width):
            row = lines[line : line + 1, first : min(first + width, tile)]
            if row.shape[1] < width:
                row = jnp.concatenate([row, jnp.zeros((1, width - row.shape[1]), jnp.float32)], axis=1)
            rows.append(row)
    rows.append(jnp.broadcast_to(over, (1, width)))
    rows.append(jnp.zeros((EXTRA - len(rows), width), jnp.float32))
    return jnp.concatenate(rows, axis=0)


def rank_lines(head_ref, tile):
    width = head_ref.shape[1]
    tail = head_ref[0:EXTRA, :].astype(jnp.float32)
    pieces = -(-tile // width)
    lines = [
        jnp.concatenate([tail[pieces * line + p : pieces * line + p + 1] for p in range(pieces)], axis=1)[:, :tile]
        for line in range(2)
    ]
    return lines[0], lines[1], tail[2 * pieces : 2 * pieces + 1, :128]


def route_kernel(cuts, home_ref, rows_hbm_ref, bucket_hbm_ref, rank_hbm_ref, *refs):
    *out_refs, rows_ref, bucket_ref, rank_ref, copied = refs
    sources = (bucket_hbm_ref, rank_hbm_ref, rows_hbm_ref)
    targets = (bucket_ref, rank_ref, rows_ref)
    copies = [pltpu.make_async_copy(*pair, copied.at[place]) for place, pair in enumerate(zip(sources, targets))]
    for copy in copies:
        copy.start()
    row_count, width = rows_ref.shape
    chunks, tile = len(cuts), sum(cuts[0])
    used = lead(tile, width)
    copies[0].wait()
    distance = (bucket_ref[...] // SHARDS) ^ home_ref[0]
    lines, span = max(chunks, 16), 256
    earlier = lax.broadcasted_iota(jnp.int32, (span, span), 0) < lax.broadcasted_iota(jnp.int32, (span, span), 1)
    earlier = jnp.where(earlier, 1.0, 0.0).astype(jnp.bfloat16)
    member = lax.broadcasted_iota(jnp.int32, (lines, row_count), 0) == distance
    member = jnp.where(member, 1.0, 0.0)
    past, places = jnp.zeros((lines, 1), jnp.float32), []
    for first in range(0, row_count, span):
        some = member[:, first : first + span]
        before = jnp.dot(some.astype(jnp.bfloat16), earlier, preferred_element_type=jnp.float32) + past
        places.append(jnp.sum(before * some, axis=0, keepdims=True))
        past += jnp.sum(some, axis=1, keepdims=True)
    place = jnp.concatenate(places, axis=1)
    over = jnp.where(jnp.max(past, axis=0, keepdims=True) > tile - used, 1.0, 0.0)
    keys = jnp.where(place < tile - used, distance * tile + place.astype(jnp.int32) + used, -1)
    out_refs[-1][...] = keys
    copies[1].wait()
    ranks = rank_ref[...]
    digit = lax.broadcasted_iota(jnp.int32, (EXTRA, row_count), 0)
    high = (ranks // 256 - 256).astype(jnp.float32)
    low = (ranks % 256).astype(jnp.float32)
    digits = jnp.where(digit == 0, high, jnp.where(digit == 1, low, 0.0)).astype(jnp.bfloat16)
    copies[2].wait()
    widened = rows_ref[...].astype(jnp.float32)
    total = jnp.sum(widened * widened, axis=1, keepdims=True) + 1e-06
    unit = (widened * lax.rsqrt(total)).astype(jnp.bfloat16)
    turned = jnp.transpose(digits.astype(jnp.float32)).astype(jnp.bfloat16)
    turned = jnp.concatenate([turned, jnp.zeros((row_count, 128 - EXTRA), jnp.bfloat16)], axis=1)
    unit = jnp.concatenate([unit, turned], axis=1)
    pieces = iter(out_refs)
    for chunk in range(chunks):
        chosen = one_hot(keys, chunk * tile, tile)
        both = jnp.dot(chosen, unit, preferred_element_type=jnp.float32)
        moved = both[:, :width].astype(jnp.bfloat16)
        first = 0
        for rows in cuts[chunk]:
            piece = next(pieces)
            piece[...] = moved[first : first + rows, :]
            if first == 0:
                tail = fold_lines(jnp.transpose(both[:, width:])[:EXTRA], over, width).astype(jnp.bfloat16)
                is_lead = lax.broadcasted_iota(jnp.int32, (EXTRA, width), 0) < used
                piece[0:EXTRA, :] = jnp.where(is_lead, tail, moved[0:EXTRA, :])
            first += rows


def route(cuts, embeddings, buckets, ranks, home):
    row_count, width = embeddings.shape
    smem = pl.BlockSpec(memory_space=pltpu.SMEM)
    vmem = pl.BlockSpec(memory_space=pltpu.VMEM)
    shapes = [jax.ShapeDtypeStruct((rows, width), jnp.bfloat16) for cut in cuts for rows in cut]
    *pieces, keys = pl.pallas_call(
        functools.partial(route_kernel, cuts),
        out_shape=shapes + [jax.ShapeDtypeStruct((1, row_count), jnp.int32)],
        in_specs=[smem] + [pl.BlockSpec(memory_space=pl.ANY)] * 3,
        out_specs=[vmem] * (len(shapes) + 1),
        scratch_shapes=[
            pltpu.VMEM((row_count, width), jnp.bfloat16),
            pltpu.VMEM((1, row_count), jnp.int32),
            pltpu.VMEM((1, row_count), jnp.int32),
            pltpu.SemaphoreType.DMA((3,)),
        ],
        compiler_params=pltpu.CompilerParams(vmem_limit_bytes=ROUTE_VMEM_LIMIT),
        name="route",
    )(home, embeddings, buckets.reshape(1, row_count), ranks.reshape(1, row_count))
    pieces = iter(pieces)
    return [[next(pieces) for _ in cut] for cut in cuts], keys


def spread_ranks(head_ref, tile, offset, target_ref, first, rows):
    high, low, _ = rank_lines(head_ref, tile)
    same = lax.broadcasted_iota(jnp.int32, (128, 128), 0) == lax.broadcasted_iota(jnp.int32, (128, 128), 1)
    ones = jnp.ones((256, 128), jnp.bfloat16)
    for block in range(0, rows, 128):
        lanes = slice(offset + block, offset + block + 128)
        diagonal = jnp.concatenate(
            [jnp.where(same, high[:, lanes] * 256.0, 0.0), jnp.where(same, low[:, lanes], 0.0)], axis=1
        ).astype(jnp.bfloat16)
        spread = jnp.dot(diagonal, ones, preferred_element_type=jnp.float32) + PAD_RANK
        target_ref[first + block : first + block + 128, :] = spread


def fold(best, query, query_rank, column_ref, column_rank):
    scores = dot_nt(column_ref[...], query)
    lanes = query.shape[0]
    column_rank = jnp.concatenate([column_rank] * (lanes // 128), axis=1)
    scores = jnp.where(column_rank < query_rank, scores, -1.0)
    return jnp.maximum(best, jnp.max(scores.reshape(-1, 8, lanes), axis=0))


def compare_kernel(plan, *refs):
    tile, queries, columns, jobs, has_held, has_best, has_over, keep, split, piece_count, lane_count = plan
    refs = iter(refs)
    piece_refs = [next(refs) for _ in range(piece_count)]
    held_refs = [next(refs) for _ in range(2 * has_held)]
    start_ref = next(refs) if has_best else None
    past_ref = next(refs) if has_over else None
    out_refs = [next(refs) for _ in range(lane_count // tile if split else 1)]
    over_ref = next(refs)
    query_ref, query_rank_ref = held_refs if has_held else (next(refs), next(refs))
    spread_ref, best_ref = refs

    over = past_ref[...].astype(jnp.float32) if has_over else jnp.zeros((1, 128), jnp.float32)
    spans, first = [], 0
    for head, piece, offset in columns:
        rows = piece_refs[piece].shape[0]
        if offset == 0:
            over = jnp.maximum(over, rank_lines(piece_refs[head], tile)[2])
        spread_ranks(piece_refs[head], tile, offset, spread_ref, first, rows)
        spans.append((piece_refs[piece], first, first + rows))
        first += rows
    over_ref[...] = over.astype(jnp.int32)

    first = 0
    for query in queries:
        high, low, _ = rank_lines(piece_refs[query[0]], tile)
        query_rank_ref[:, first : first + tile] = high * 256.0 + low + PAD_RANK
        for piece in query:
            rows = piece_refs[piece].shape[0]
            query_ref[first : first + rows, :] = piece_refs[piece][...]
            first += rows
    best_ref[...] = jnp.full((1, lane_count), -1.0, jnp.float32)
    if has_best:
        best_ref[:, : start_ref.shape[1]] = start_ref[...]

    for lane_from, lane_to, column_from, column_to in jobs:
        rows = sum(stop - start for _, start, stop in spans[column_from:column_to])
        width = lane_to - lane_from if (lane_to - lane_from) * rows <= WHOLE else LANES

        def one_tile(step, carry, width=width, lane_from=lane_from, column_from=column_from, column_to=column_to):
            lanes = pl.ds(pl.multiple_of(lane_from + step * width, 128), width)
            query = query_ref[lanes, :]
            query_rank = query_rank_ref[:, lanes]
            best = jnp.broadcast_to(best_ref[:, lanes], (8, width))
            for column_ref, start, stop in spans[column_from:column_to]:
                best = fold(best, query, query_rank, column_ref, spread_ref[start:stop, :])
            best_ref[:, lanes] = jnp.max(best, axis=0, keepdims=True)
            return carry

        lax.fori_loop(0, (lane_to - lane_from) // width, one_tile, 0)
    if split:
        for place, out_ref in enumerate(out_refs):
            out_ref[...] = best_ref[:, place * tile : place * tile + tile]
    else:
        out_refs[0][...] = best_ref[...]


def columns_of(block):
    first, out = 0, []
    for piece in block:
        out.append((block[0], piece, first))
        first += piece.shape[0]
    return out


def compare(tile, columns, jobs, queries=(), held=(), best=None, over=None, keep=False, split=False):
    pieces = []

    def index_of(array):
        for place, other in enumerate(pieces):
            if other is array:
                return place
        pieces.append(array)
        return len(pieces) - 1

    column_plan = tuple((index_of(head), index_of(piece), offset) for head, piece, offset in columns)
    query_plan = tuple(tuple(index_of(piece) for piece in block) for block in queries)
    lane_count = held[0].shape[0] if held else len(queries) * tile
    width = pieces[0].shape[1]
    plan = (
        tile, query_plan, column_plan, tuple(jobs), bool(held), best is not None, over is not None, keep, split,
        len(pieces), lane_count,
    )
    operands = pieces + list(held) + [array for array in (best, over) if array is not None]
    query_shapes = [((lane_count, width), jnp.bfloat16), ((1, lane_count), jnp.float32)]
    lines = lane_count // tile if split else 1
    outs = [jax.ShapeDtypeStruct((1, lane_count // lines), jnp.float32)] * lines
    outs.append(jax.ShapeDtypeStruct((1, 128), jnp.int32))
    scratch = []
    if keep:
        outs += [jax.ShapeDtypeStruct(*shape) for shape in query_shapes]
    elif not held:
        scratch += [pltpu.VMEM(*shape) for shape in query_shapes]
    column_rows = sum(piece.shape[0] for _, piece, _ in columns)
    scratch += [pltpu.VMEM((column_rows, 128), jnp.float32), pltpu.VMEM((1, lane_count), jnp.float32)]
    vmem = pl.BlockSpec(memory_space=pltpu.VMEM)
    results = pl.pallas_call(
        functools.partial(compare_kernel, plan),
        out_shape=outs,
        in_specs=[vmem] * len(operands),
        out_specs=[vmem] * len(outs),
        scratch_shapes=scratch,
        compiler_params=pltpu.CompilerParams(vmem_limit_bytes=VMEM_LIMIT),
        name="compare",
    )(*operands)
    found = results[:lines] if split else results[0]
    return found, results[lines], results[lines + 1 :]


def place_kernel(chunks, tile, key_ref, *refs):
    keys = key_ref[...]
    out_ref = refs[-1]
    gathered = jnp.zeros((16, keys.shape[1]), jnp.float32)
    line = lax.broadcasted_iota(jnp.int32, (16, tile), 0)
    for chunk in range(chunks):
        value = refs[chunk][...]
        first = value.astype(jnp.bfloat16).astype(jnp.float32)
        second = (value - first).astype(jnp.bfloat16).astype(jnp.float32)
        third = value - first - second
        parts = jnp.where(line == 0, first, jnp.where(line == 1, second, jnp.where(line == 2, third, 0.0)))
        gathered += jnp.dot(
            parts.astype(jnp.bfloat16), one_hot(keys, chunk * tile, tile), preferred_element_type=jnp.float32
        )
    found = jnp.sum(gathered, axis=0, keepdims=True)
    if len(refs) > chunks + 1:
        over_ref, roomy_ref = refs[chunks : chunks + 2]
        found = jnp.where(over_ref[:, :1] > 0, roomy_ref[...], found)
    out_ref[...] = found


def place(chunks, tile, keys, values, *instead):
    vmem = pl.BlockSpec(memory_space=pltpu.VMEM)
    return pl.pallas_call(
        functools.partial(place_kernel, chunks, tile),
        out_shape=jax.ShapeDtypeStruct(keys.shape, jnp.float32),
        in_specs=[vmem] * (chunks + 1 + len(instead)),
        out_specs=vmem,
        compiler_params=pltpu.CompilerParams(vmem_limit_bytes=VMEM_LIMIT),
        name="place",
    )(keys, *values, *instead)


def swap(block, mask):
    return [from_partner(piece, "owners", mask) for piece in block]


def after(value, *others):
    return lax.optimization_barrier((value, *others))[0]


def give_back(chunks, tile, keys, best, *instead):
    returned = [best[0]] + [from_partner(best[k], "owners", SHARDS * k) for k in range(1, chunks)]
    return place(chunks, tile, keys, returned, *instead).reshape(keys.shape[1])


def roomy(chunks, tile, embeddings, buckets, ranks, home):
    sent, keys = route(((tile,),) * chunks, embeddings, buckets, ranks, home)
    own = [sent[0]] + [swap(sent[k], SHARDS * k) for k in range(1, chunks)]
    pair = own + [swap(block, 1) for block in own]
    lanes = chunks * tile
    columns = sum(map(columns_of, pair), [])
    best, over, held = compare(tile, columns, ((0, lanes, 0, len(columns)),), own, keep=True)
    columns = sum((columns_of(swap(block, 2)) for block in pair), [])
    best, *_ = compare(tile, columns, ((0, lanes, 0, len(columns)),), held=held, best=best, split=True)
    return give_back(chunks, tile, keys, best)


def snug(chunks, tile, embeddings, buckets, ranks, home):
    sent, keys = route(((tile,),) * chunks, embeddings, buckets, ranks, home)
    lanes, wave = chunks * tile, chunks // 4
    first_lanes = 3 * wave * tile // LANES * LANES

    def hop(blocks, mask, *others):
        return [swap([after(piece, *others) for piece in block] if others else block, mask) for block in blocks]

    def z_hop(place, *others):
        group = range(place * wave, place * wave + wave)
        return sum((hop(sent[k : k + 1], SHARDS * k, *others) if k else sent[:1] for k in group), [])

    def columns(*groups):
        return sum(map(columns_of, sum(groups, [])), [])

    z0 = z_hop(0)
    z1 = z_hop(1)
    z2 = z_hop(2)
    z3 = z_hop(3)
    y0 = hop(z0, 2)
    c0 = hop(z0, 1, z1[0][0])
    d0 = hop(y0, 1)
    y1 = hop(z1, 2)
    y2 = hop(z2, 2)
    seen = columns(z0, z1, z2, y0, c0, d0)
    k1, over, _ = compare(tile, seen, ((0, first_lanes, 0, len(seen)),), z0 + z1 + z2)
    c1 = hop(z1, 1, z1[0][0])
    c2 = hop(z2, 1, z2[0][0])
    d1 = hop(y1, 1, k1)
    z3 = [[after(piece, k1) for piece in block] for block in z3]
    y3 = hop(z3, 2)
    c3 = hop(z3, 1)
    d2 = hop(y2, 1)
    every = seen + columns(z3, y2, c3, d2, c1, c2, y1, d1)
    jobs = ((first_lanes, lanes, 0, len(seen)), (0, lanes, len(seen), len(every)))
    k2, over, held = compare(tile, every, jobs, z0 + z1 + z2 + z3, best=k1, over=over, keep=True)
    y3 = [[after(piece, k2) for piece in block] for block in y3]
    d3 = hop(y3, 1)
    late = columns(y3)
    k3, over, _ = compare(tile, late, ((0, lanes, 0, len(late)),), held=held, best=k2, over=over)
    last = columns(d3)
    best, over, _ = compare(tile, last, ((0, lanes, 0, len(last)),), held=held, best=k3, over=over, split=True)
    return keys, best, over


def body(embeddings, buckets, ranks):
    chunks = lax.axis_size("owners") // SHARDS
    full = SHARDS * 2 * embeddings.shape[0] // lax.axis_size("owners")
    tile = -(-(3 * full // 4) // 128) * 128
    roomy_tile = -(-(full + EXTRA) // 128) * 128
    home = (lax.axis_index("owners") // SHARDS).astype(jnp.int32).reshape(1)
    operands = (embeddings, buckets, ranks, home)
    keys, best, over = snug(chunks, tile, *operands)
    other = lax.cond(
        over[0, 0] > 0,
        functools.partial(roomy, chunks, roomy_tile),
        lambda embeddings, *_: jnp.zeros((embeddings.shape[0],), jnp.float32),
        *operands,
    )
    return give_back(chunks, tile, keys, best, over, other.reshape(keys.shape))


def solution(mesh):
    in_specs = (P(("groups", "owners"), None), P(("groups", "owners")), P(("groups", "owners")))
    out_specs = P(("groups", "owners"))
    return jax.shard_map(body, mesh=mesh, in_specs=in_specs, out_specs=out_specs, check_vma=False)
```

```python
import functools

import jax
import jax.numpy as jnp
from jax import lax
from jax.experimental import pallas as pl
from jax.experimental.pallas import tpu as pltpu
from jax.sharding import PartitionSpec as P

SHARDS = 4
EXTRA = 16
PAD_RANK = 65536.0
LANES = 512
WHOLE = 5 * 1024 * 1024
VMEM_LIMIT = 48 * 1024 * 1024
ROUTE_VMEM_LIMIT = 60 * 1024 * 1024


def from_partner(value, axis, mask):
    pairs = [(source, source ^ mask) for source in range(lax.axis_size(axis))]
    return lax.ppermute(value, axis, pairs)


def dot_nt(left, right):
    return lax.dot_general(left, right, (((1,), (1,)), ((), ())), preferred_element_type=jnp.float32)


def one_hot(keys, first, count):
    rows = lax.broadcasted_iota(jnp.int32, (count, keys.shape[1]), 0) + first
    return jnp.where(rows == keys, 1.0, 0.0).astype(jnp.bfloat16)


def lead(tile, width):
    return 2 * -(-tile // width) + 1


def fold_lines(lines, over, width):
    tile = lines.shape[1]
    rows = []
    for line in range(2):
        for first in range(0, tile, width):
            row = lines[line : line + 1, first : min(first + width, tile)]
            if row.shape[1] < width:
                row = jnp.concatenate([row, jnp.zeros((1, width - row.shape[1]), jnp.float32)], axis=1)
            rows.append(row)
    rows.append(jnp.broadcast_to(over, (1, width)))
    rows.append(jnp.zeros((EXTRA - len(rows), width), jnp.float32))
    return jnp.concatenate(rows, axis=0)


def rank_lines(head_ref, tile):
    width = head_ref.shape[1]
    tail = head_ref[0:EXTRA, :].astype(jnp.float32)
    pieces = -(-tile // width)
    lines = [
        jnp.concatenate([tail[pieces * line + p : pieces * line + p + 1] for p in range(pieces)], axis=1)[:, :tile]
        for line in range(2)
    ]
    return lines[0], lines[1], tail[2 * pieces : 2 * pieces + 1, :128]


def route_kernel(cuts, home_ref, rows_hbm_ref, bucket_hbm_ref, rank_hbm_ref, *refs):
    *out_refs, rows_ref, bucket_ref, rank_ref, copied = refs
    sources = (bucket_hbm_ref, rank_hbm_ref, rows_hbm_ref)
    targets = (bucket_ref, rank_ref, rows_ref)
    copies = [pltpu.make_async_copy(*pair, copied.at[place]) for place, pair in enumerate(zip(sources, targets))]
    for copy in copies:
        copy.start()
    row_count, width = rows_ref.shape
    chunks, tile = len(cuts), sum(cuts[0])
    used = lead(tile, width)
    copies[0].wait()
    distance = (bucket_ref[...] // SHARDS) ^ home_ref[0]
    lines, span = max(chunks, 16), 256
    earlier = lax.broadcasted_iota(jnp.int32, (span, span), 0) < lax.broadcasted_iota(jnp.int32, (span, span), 1)
    earlier = jnp.where(earlier, 1.0, 0.0).astype(jnp.bfloat16)
    member = lax.broadcasted_iota(jnp.int32, (lines, row_count), 0) == distance
    member = jnp.where(member, 1.0, 0.0)
    past, places = jnp.zeros((lines, 1), jnp.float32), []
    for first in range(0, row_count, span):
        some = member[:, first : first + span]
        before = jnp.dot(some.astype(jnp.bfloat16), earlier, preferred_element_type=jnp.float32) + past
        places.append(jnp.sum(before * some, axis=0, keepdims=True))
        past += jnp.sum(some, axis=1, keepdims=True)
    place = jnp.concatenate(places, axis=1)
    over = jnp.where(jnp.max(past, axis=0, keepdims=True) > tile - used, 1.0, 0.0)
    keys = jnp.where(place < tile - used, distance * tile + place.astype(jnp.int32) + used, -1)
    out_refs[-1][...] = keys
    copies[1].wait()
    ranks = rank_ref[...]
    digit = lax.broadcasted_iota(jnp.int32, (EXTRA, row_count), 0)
    high = (ranks // 256 - 256).astype(jnp.float32)
    low = (ranks % 256).astype(jnp.float32)
    digits = jnp.where(digit == 0, high, jnp.where(digit == 1, low, 0.0)).astype(jnp.bfloat16)
    copies[2].wait()
    widened = rows_ref[...].astype(jnp.float32)
    total = jnp.sum(widened * widened, axis=1, keepdims=True) + 1e-06
    unit = (widened * lax.rsqrt(total)).astype(jnp.bfloat16)
    turned = jnp.transpose(digits.astype(jnp.float32)).astype(jnp.bfloat16)
    turned = jnp.concatenate([turned, jnp.zeros((row_count, 128 - EXTRA), jnp.bfloat16)], axis=1)
    unit = jnp.concatenate([unit, turned], axis=1)
    pieces = iter(out_refs)
    for chunk in range(chunks):
        chosen = one_hot(keys, chunk * tile, tile)
        both = jnp.dot(chosen, unit, preferred_element_type=jnp.float32)
        moved = both[:, :width].astype(jnp.bfloat16)
        first = 0
        for rows in cuts[chunk]:
            piece = next(pieces)
            piece[...] = moved[first : first + rows, :]
            if first == 0:
                tail = fold_lines(jnp.transpose(both[:, width:])[:EXTRA], over, width).astype(jnp.bfloat16)
                is_lead = lax.broadcasted_iota(jnp.int32, (EXTRA, width), 0) < used
                piece[0:EXTRA, :] = jnp.where(is_lead, tail, moved[0:EXTRA, :])
            first += rows


def route(cuts, embeddings, buckets, ranks, home):
    row_count, width = embeddings.shape
    smem = pl.BlockSpec(memory_space=pltpu.SMEM)
    vmem = pl.BlockSpec(memory_space=pltpu.VMEM)
    shapes = [jax.ShapeDtypeStruct((rows, width), jnp.bfloat16) for cut in cuts for rows in cut]
    *pieces, keys = pl.pallas_call(
        functools.partial(route_kernel, cuts),
        out_shape=shapes + [jax.ShapeDtypeStruct((1, row_count), jnp.int32)],
        in_specs=[smem] + [pl.BlockSpec(memory_space=pl.ANY)] * 3,
        out_specs=[vmem] * (len(shapes) + 1),
        scratch_shapes=[
            pltpu.VMEM((row_count, width), jnp.bfloat16),
            pltpu.VMEM((1, row_count), jnp.int32),
            pltpu.VMEM((1, row_count), jnp.int32),
            pltpu.SemaphoreType.DMA((3,)),
        ],
        compiler_params=pltpu.CompilerParams(vmem_limit_bytes=ROUTE_VMEM_LIMIT),
        name="route",
    )(home, embeddings, buckets.reshape(1, row_count), ranks.reshape(1, row_count))
    pieces = iter(pieces)
    return [[next(pieces) for _ in cut] for cut in cuts], keys


def spread_ranks(head_ref, tile, offset, target_ref, first, rows):
    high, low, _ = rank_lines(head_ref, tile)
    same = lax.broadcasted_iota(jnp.int32, (128, 128), 0) == lax.broadcasted_iota(jnp.int32, (128, 128), 1)
    ones = jnp.ones((256, 128), jnp.bfloat16)
    for block in range(0, rows, 128):
        lanes = slice(offset + block, offset + block + 128)
        diagonal = jnp.concatenate(
            [jnp.where(same, high[:, lanes] * 256.0, 0.0), jnp.where(same, low[:, lanes], 0.0)], axis=1
        ).astype(jnp.bfloat16)
        spread = jnp.dot(diagonal, ones, preferred_element_type=jnp.float32) + PAD_RANK
        target_ref[first + block : first + block + 128, :] = spread


def fold(best, query, query_rank, column_ref, column_rank):
    scores = dot_nt(column_ref[...], query)
    lanes = query.shape[0]
    column_rank = jnp.concatenate([column_rank] * (lanes // 128), axis=1)
    scores = jnp.where(column_rank < query_rank, scores, -1.0)
    return jnp.maximum(best, jnp.max(scores.reshape(-1, 8, lanes), axis=0))


def compare_kernel(plan, *refs):
    tile, queries, columns, jobs, has_held, has_best, has_over, keep, split, piece_count, lane_count = plan
    refs = iter(refs)
    piece_refs = [next(refs) for _ in range(piece_count)]
    held_refs = [next(refs) for _ in range(2 * has_held)]
    start_ref = next(refs) if has_best else None
    past_ref = next(refs) if has_over else None
    out_refs = [next(refs) for _ in range(lane_count // tile if split else 1)]
    over_ref = next(refs)
    query_ref, query_rank_ref = held_refs if has_held else (next(refs), next(refs))
    spread_ref, best_ref = refs

    over = past_ref[...].astype(jnp.float32) if has_over else jnp.zeros((1, 128), jnp.float32)
    spans, first = [], 0
    for head, piece, offset in columns:
        rows = piece_refs[piece].shape[0]
        if offset == 0:
            over = jnp.maximum(over, rank_lines(piece_refs[head], tile)[2])
        spread_ranks(piece_refs[head], tile, offset, spread_ref, first, rows)
        spans.append((piece_refs[piece], first, first + rows))
        first += rows
    over_ref[...] = over.astype(jnp.int32)

    first = 0
    for query in queries:
        high, low, _ = rank_lines(piece_refs[query[0]], tile)
        query_rank_ref[:, first : first + tile] = high * 256.0 + low + PAD_RANK
        for piece in query:
            rows = piece_refs[piece].shape[0]
            query_ref[first : first + rows, :] = piece_refs[piece][...]
            first += rows
    best_ref[...] = jnp.full((1, lane_count), -1.0, jnp.float32)
    if has_best:
        best_ref[:, : start_ref.shape[1]] = start_ref[...]

    for lane_from, lane_to, column_from, column_to in jobs:
        rows = sum(stop - start for _, start, stop in spans[column_from:column_to])
        width = lane_to - lane_from if (lane_to - lane_from) * rows <= WHOLE else LANES

        def one_tile(step, carry, width=width, lane_from=lane_from, column_from=column_from, column_to=column_to):
            lanes = pl.ds(pl.multiple_of(lane_from + step * width, 128), width)
            query = query_ref[lanes, :]
            query_rank = query_rank_ref[:, lanes]
            best = jnp.broadcast_to(best_ref[:, lanes], (8, width))
            for column_ref, start, stop in spans[column_from:column_to]:
                best = fold(best, query, query_rank, column_ref, spread_ref[start:stop, :])
            best_ref[:, lanes] = jnp.max(best, axis=0, keepdims=True)
            return carry

        lax.fori_loop(0, (lane_to - lane_from) // width, one_tile, 0)
    if split:
        for place, out_ref in enumerate(out_refs):
            out_ref[...] = best_ref[:, place * tile : place * tile + tile]
    else:
        out_refs[0][...] = best_ref[...]


def columns_of(block):
    first, out = 0, []
    for piece in block:
        out.append((block[0], piece, first))
        first += piece.shape[0]
    return out


def compare(tile, columns, jobs, queries=(), held=(), best=None, over=None, keep=False, split=False):
    pieces = []

    def index_of(array):
        for place, other in enumerate(pieces):
            if other is array:
                return place
        pieces.append(array)
        return len(pieces) - 1

    column_plan = tuple((index_of(head), index_of(piece), offset) for head, piece, offset in columns)
    query_plan = tuple(tuple(index_of(piece) for piece in block) for block in queries)
    lane_count = held[0].shape[0] if held else len(queries) * tile
    width = pieces[0].shape[1]
    plan = (
        tile, query_plan, column_plan, tuple(jobs), bool(held), best is not None, over is not None, keep, split,
        len(pieces), lane_count,
    )
    operands = pieces + list(held) + [array for array in (best, over) if array is not None]
    query_shapes = [((lane_count, width), jnp.bfloat16), ((1, lane_count), jnp.float32)]
    lines = lane_count // tile if split else 1
    outs = [jax.ShapeDtypeStruct((1, lane_count // lines), jnp.float32)] * lines
    outs.append(jax.ShapeDtypeStruct((1, 128), jnp.int32))
    scratch = []
    if keep:
        outs += [jax.ShapeDtypeStruct(*shape) for shape in query_shapes]
    elif not held:
        scratch += [pltpu.VMEM(*shape) for shape in query_shapes]
    column_rows = sum(piece.shape[0] for _, piece, _ in columns)
    scratch += [pltpu.VMEM((column_rows, 128), jnp.float32), pltpu.VMEM((1, lane_count), jnp.float32)]
    vmem = pl.BlockSpec(memory_space=pltpu.VMEM)
    results = pl.pallas_call(
        functools.partial(compare_kernel, plan),
        out_shape=outs,
        in_specs=[vmem] * len(operands),
        out_specs=[vmem] * len(outs),
        scratch_shapes=scratch,
        compiler_params=pltpu.CompilerParams(vmem_limit_bytes=VMEM_LIMIT),
        name="compare",
    )(*operands)
    found = results[:lines] if split else results[0]
    return found, results[lines], results[lines + 1 :]


def place_kernel(chunks, tile, key_ref, *refs):
    keys = key_ref[...]
    out_ref = refs[-1]
    gathered = jnp.zeros((16, keys.shape[1]), jnp.float32)
    line = lax.broadcasted_iota(jnp.int32, (16, tile), 0)
    for chunk in range(chunks):
        value = refs[chunks - 1 - chunk][...]
        first = value.astype(jnp.bfloat16).astype(jnp.float32)
        second = (value - first).astype(jnp.bfloat16).astype(jnp.float32)
        third = value - first - second
        parts = jnp.where(line == 0, first, jnp.where(line == 1, second, jnp.where(line == 2, third, 0.0)))
        gathered += jnp.dot(
            parts.astype(jnp.bfloat16), one_hot(keys, chunk * tile, tile), preferred_element_type=jnp.float32
        )
    found = jnp.sum(gathered, axis=0, keepdims=True)
    if len(refs) > chunks + 1:
        over_ref, roomy_ref = refs[chunks : chunks + 2]
        found = jnp.where(over_ref[:, :1] > 0, roomy_ref[...], found)
    out_ref[...] = found


def place(chunks, tile, keys, values, *instead):
    vmem = pl.BlockSpec(memory_space=pltpu.VMEM)
    return pl.pallas_call(
        functools.partial(place_kernel, chunks, tile),
        out_shape=jax.ShapeDtypeStruct(keys.shape, jnp.float32),
        in_specs=[vmem] * (chunks + 1 + len(instead)),
        out_specs=vmem,
        compiler_params=pltpu.CompilerParams(vmem_limit_bytes=VMEM_LIMIT),
        name="place",
    )(keys, *reversed(values), *instead)


def swap(block, mask):
    return [from_partner(piece, "owners", mask) for piece in block]


def after(value, *others):
    return lax.optimization_barrier((value, *others))[0]


def give_back(chunks, tile, keys, best, *instead):
    returned = [best[0]] + [from_partner(best[k], "owners", SHARDS * k) for k in range(1, chunks)]
    return place(chunks, tile, keys, returned, *instead).reshape(keys.shape[1])


def roomy(chunks, tile, embeddings, buckets, ranks, home):
    sent, keys = route(((tile,),) * chunks, embeddings, buckets, ranks, home)
    own = [sent[0]] + [swap(sent[k], SHARDS * k) for k in range(1, chunks)]
    pair = own + [swap(block, 1) for block in own]
    lanes = chunks * tile
    columns = sum(map(columns_of, pair), [])
    best, over, held = compare(tile, columns, ((0, lanes, 0, len(columns)),), own, keep=True)
    columns = sum((columns_of(swap(block, 2)) for block in pair), [])
    best, *_ = compare(tile, columns, ((0, lanes, 0, len(columns)),), held=held, best=best, split=True)
    return give_back(chunks, tile, keys, best)


def snug(chunks, tile, embeddings, buckets, ranks, home):
    sent, keys = route(((tile,),) * chunks, embeddings, buckets, ranks, home)
    lanes, wave = chunks * tile, chunks // 4
    first_lanes = 3 * wave * tile // LANES * LANES

    def hop(blocks, mask, *others):
        return [swap([after(piece, *others) for piece in block] if others else block, mask) for block in blocks]

    def z_hop(place, *others):
        group = range(place * wave, place * wave + wave)
        return sum((hop(sent[k : k + 1], SHARDS * k, *others) if k else sent[:1] for k in group), [])

    def columns(*groups):
        return sum(map(columns_of, sum(groups, [])), [])

    z0 = z_hop(0)
    z1 = z_hop(1)
    z2 = z_hop(2)
    z3 = z_hop(3)
    y0 = hop(z0, 2)
    c0 = hop(z0, 1, z1[0][0])
    d0 = hop(y0, 1)
    y1 = hop(z1, 2)
    y2 = hop(z2, 2)
    seen = columns(z0, z1, z2, y0, c0, d0)
    k1, over, _ = compare(tile, seen, ((0, first_lanes, 0, len(seen)),), z0 + z1 + z2)
    c1 = hop(z1, 1, z1[0][0])
    c2 = hop(z2, 1, z2[0][0])
    d1 = hop(y1, 1, k1)
    z3 = [[after(piece, k1) for piece in block] for block in z3]
    y3 = hop(z3, 2)
    c3 = hop(z3, 1)
    d2 = hop(y2, 1)
    every = seen + columns(z3, y2, c3, d2, c1, c2, y1, d1)
    jobs = ((first_lanes, lanes, 0, len(seen)), (0, lanes, len(seen), len(every)))
    k2, over, held = compare(tile, every, jobs, z0 + z1 + z2 + z3, best=k1, over=over, keep=True)
    y3 = [[after(piece, k2) for piece in block] for block in y3]
    d3 = hop(y3, 1)
    late = columns(y3)
    k3, over, _ = compare(tile, late, ((0, lanes, 0, len(late)),), held=held, best=k2, over=over)
    last = columns(d3)
    best, over, _ = compare(tile, last, ((0, lanes, 0, len(last)),), held=held, best=k3, over=over, split=True)
    return keys, best, over


def body(embeddings, buckets, ranks):
    chunks = lax.axis_size("owners") // SHARDS
    full = SHARDS * 2 * embeddings.shape[0] // lax.axis_size("owners")
    tile = -(-(3 * full // 4) // 128) * 128
    roomy_tile = -(-(full + EXTRA) // 128) * 128
    home = (lax.axis_index("owners") // SHARDS).astype(jnp.int32).reshape(1)
    operands = (embeddings, buckets, ranks, home)
    keys, best, over = snug(chunks, tile, *operands)
    other = lax.cond(
        over[0, 0] > 0,
        functools.partial(roomy, chunks, roomy_tile),
        lambda embeddings, *_: jnp.zeros((embeddings.shape[0],), jnp.float32),
        *operands,
    )
    return give_back(chunks, tile, keys, best, over, other.reshape(keys.shape))


def solution(mesh):
    in_specs = (P(("groups", "owners"), None), P(("groups", "owners")), P(("groups", "owners")))
    out_specs = P(("groups", "owners"))
    return jax.shard_map(body, mesh=mesh, in_specs=in_specs, out_specs=out_specs, check_vma=False)
```

```python
import functools

import jax
import jax.numpy as jnp
from jax import lax
from jax.experimental import pallas as pl
from jax.experimental.pallas import tpu as pltpu
from jax.sharding import PartitionSpec as P

SHARDS = 4
EXTRA = 16
PAD_RANK = 65536.0
LANES = 512
WHOLE = 5 * 1024 * 1024
VMEM_LIMIT = 48 * 1024 * 1024
ROUTE_VMEM_LIMIT = 48 * 1024 * 1024


def from_partner(value, axis, mask):
    pairs = [(source, source ^ mask) for source in range(lax.axis_size(axis))]
    return lax.ppermute(value, axis, pairs)


def dot_nt(left, right):
    return lax.dot_general(left, right, (((1,), (1,)), ((), ())), preferred_element_type=jnp.float32)


def one_hot(keys, first, count):
    rows = lax.broadcasted_iota(jnp.int32, (count, keys.shape[1]), 0) + first
    return jnp.where(rows == keys, 1.0, 0.0).astype(jnp.bfloat16)


def lead(tile, width):
    return 2 * -(-tile // width) + 1


def fold_lines(lines, over, width):
    tile = lines.shape[1]
    rows = []
    for line in range(2):
        for first in range(0, tile, width):
            row = lines[line : line + 1, first : min(first + width, tile)]
            if row.shape[1] < width:
                row = jnp.concatenate([row, jnp.zeros((1, width - row.shape[1]), jnp.float32)], axis=1)
            rows.append(row)
    rows.append(jnp.broadcast_to(over, (1, width)))
    rows.append(jnp.zeros((EXTRA - len(rows), width), jnp.float32))
    return jnp.concatenate(rows, axis=0)


def rank_lines(head_ref, tile):
    width = head_ref.shape[1]
    tail = head_ref[0:EXTRA, :].astype(jnp.float32)
    pieces = -(-tile // width)
    lines = [
        jnp.concatenate([tail[pieces * line + p : pieces * line + p + 1] for p in range(pieces)], axis=1)[:, :tile]
        for line in range(2)
    ]
    return lines[0], lines[1], tail[2 * pieces : 2 * pieces + 1, :128]


def route_kernel(cuts, home_ref, rows_hbm_ref, bucket_hbm_ref, rank_hbm_ref, *refs):
    *out_refs, rows_ref, bucket_ref, rank_ref, copied = refs
    sources = (bucket_hbm_ref, rank_hbm_ref, rows_hbm_ref)
    targets = (bucket_ref, rank_ref, rows_ref)
    copies = [pltpu.make_async_copy(*pair, copied.at[place]) for place, pair in enumerate(zip(sources, targets))]
    for copy in copies:
        copy.start()
    row_count, width = rows_ref.shape
    chunks, tile = len(cuts), sum(cuts[0])
    used = lead(tile, width)
    copies[0].wait()
    distance = (bucket_ref[...] // SHARDS) ^ home_ref[0]
    lines, span = max(chunks, 16), 256
    earlier = lax.broadcasted_iota(jnp.int32, (span, span), 0) < lax.broadcasted_iota(jnp.int32, (span, span), 1)
    earlier = jnp.where(earlier, 1.0, 0.0).astype(jnp.bfloat16)
    member = lax.broadcasted_iota(jnp.int32, (lines, row_count), 0) == distance
    member = jnp.where(member, 1.0, 0.0)
    past, places = jnp.zeros((lines, 1), jnp.float32), []
    for first in range(0, row_count, span):
        some = member[:, first : first + span]
        before = jnp.dot(some.astype(jnp.bfloat16), earlier, preferred_element_type=jnp.float32) + past
        places.append(jnp.sum(before * some, axis=0, keepdims=True))
        past += jnp.sum(some, axis=1, keepdims=True)
    place = jnp.concatenate(places, axis=1)
    over = jnp.where(jnp.max(past, axis=0, keepdims=True) > tile - used, 1.0, 0.0)
    keys = jnp.where(place < tile - used, distance * tile + place.astype(jnp.int32) + used, -1)
    out_refs[-1][...] = keys
    copies[1].wait()
    ranks = rank_ref[...]
    digit = lax.broadcasted_iota(jnp.int32, (EXTRA, row_count), 0)
    high = (ranks // 256 - 256).astype(jnp.float32)
    low = (ranks % 256).astype(jnp.float32)
    digits = jnp.where(digit == 0, high, jnp.where(digit == 1, low, 0.0)).astype(jnp.bfloat16)
    copies[2].wait()
    widened = rows_ref[...].astype(jnp.float32)
    total = jnp.sum(widened * widened, axis=1, keepdims=True) + 1e-06
    unit = (widened * lax.rsqrt(total)).astype(jnp.bfloat16)
    turned = jnp.transpose(digits.astype(jnp.float32)).astype(jnp.bfloat16)
    turned = jnp.concatenate([turned, jnp.zeros((row_count, 128 - EXTRA), jnp.bfloat16)], axis=1)
    unit = jnp.concatenate([unit, turned], axis=1)
    pieces = iter(out_refs)
    for chunk in range(chunks):
        chosen = one_hot(keys, chunk * tile, tile)
        both = jnp.dot(chosen, unit, preferred_element_type=jnp.float32)
        moved = both[:, :width].astype(jnp.bfloat16)
        first = 0
        for rows in cuts[chunk]:
            piece = next(pieces)
            piece[...] = moved[first : first + rows, :]
            if first == 0:
                tail = fold_lines(jnp.transpose(both[:, width:])[:EXTRA], over, width).astype(jnp.bfloat16)
                is_lead = lax.broadcasted_iota(jnp.int32, (EXTRA, width), 0) < used
                piece[0:EXTRA, :] = jnp.where(is_lead, tail, moved[0:EXTRA, :])
            first += rows


def route(cuts, embeddings, buckets, ranks, home):
    row_count, width = embeddings.shape
    smem = pl.BlockSpec(memory_space=pltpu.SMEM)
    vmem = pl.BlockSpec(memory_space=pltpu.VMEM)
    shapes = [jax.ShapeDtypeStruct((rows, width), jnp.bfloat16) for cut in cuts for rows in cut]
    *pieces, keys = pl.pallas_call(
        functools.partial(route_kernel, cuts),
        out_shape=shapes + [jax.ShapeDtypeStruct((1, row_count), jnp.int32)],
        in_specs=[smem] + [pl.BlockSpec(memory_space=pl.ANY)] * 3,
        out_specs=[vmem] * (len(shapes) + 1),
        scratch_shapes=[
            pltpu.VMEM((row_count, width), jnp.bfloat16),
            pltpu.VMEM((1, row_count), jnp.int32),
            pltpu.VMEM((1, row_count), jnp.int32),
            pltpu.SemaphoreType.DMA((3,)),
        ],
        compiler_params=pltpu.CompilerParams(vmem_limit_bytes=ROUTE_VMEM_LIMIT),
        name="route",
    )(home, embeddings, buckets.reshape(1, row_count), ranks.reshape(1, row_count))
    pieces = iter(pieces)
    return [[next(pieces) for _ in cut] for cut in cuts], keys


def spread_ranks(head_ref, tile, offset, target_ref, first, rows):
    high, low, _ = rank_lines(head_ref, tile)
    same = lax.broadcasted_iota(jnp.int32, (128, 128), 0) == lax.broadcasted_iota(jnp.int32, (128, 128), 1)
    ones = jnp.ones((256, 128), jnp.bfloat16)
    for block in range(0, rows, 128):
        lanes = slice(offset + block, offset + block + 128)
        diagonal = jnp.concatenate(
            [jnp.where(same, high[:, lanes] * 256.0, 0.0), jnp.where(same, low[:, lanes], 0.0)], axis=1
        ).astype(jnp.bfloat16)
        spread = jnp.dot(diagonal, ones, preferred_element_type=jnp.float32) + PAD_RANK
        target_ref[first + block : first + block + 128, :] = spread


def fold(best, query, query_rank, column_ref, column_rank):
    scores = dot_nt(column_ref[...], query)
    lanes = query.shape[0]
    column_rank = jnp.concatenate([column_rank] * (lanes // 128), axis=1)
    scores = jnp.where(column_rank < query_rank, scores, -1.0)
    return jnp.maximum(best, jnp.max(scores.reshape(-1, 8, lanes), axis=0))


def compare_kernel(plan, *refs):
    tile, queries, columns, jobs, has_held, has_best, has_over, keep, split, piece_count, lane_count = plan
    refs = iter(refs)
    piece_refs = [next(refs) for _ in range(piece_count)]
    held_refs = [next(refs) for _ in range(2 * has_held)]
    start_ref = next(refs) if has_best else None
    past_ref = next(refs) if has_over else None
    out_refs = [next(refs) for _ in range(lane_count // tile if split else 1)]
    over_ref = next(refs)
    query_ref, query_rank_ref = held_refs if has_held else (next(refs), next(refs))
    spread_ref, best_ref = refs

    over = past_ref[...].astype(jnp.float32) if has_over else jnp.zeros((1, 128), jnp.float32)
    spans, first = [], 0
    for head, piece, offset in columns:
        rows = piece_refs[piece].shape[0]
        if offset == 0:
            over = jnp.maximum(over, rank_lines(piece_refs[head], tile)[2])
        spread_ranks(piece_refs[head], tile, offset, spread_ref, first, rows)
        spans.append((piece_refs[piece], first, first + rows))
        first += rows
    over_ref[...] = over.astype(jnp.int32)

    first = 0
    for query in queries:
        high, low, _ = rank_lines(piece_refs[query[0]], tile)
        query_rank_ref[:, first : first + tile] = high * 256.0 + low + PAD_RANK
        for piece in query:
            rows = piece_refs[piece].shape[0]
            query_ref[first : first + rows, :] = piece_refs[piece][...]
            first += rows
    best_ref[...] = jnp.full((1, lane_count), -1.0, jnp.float32)
    if has_best:
        best_ref[:, : start_ref.shape[1]] = start_ref[...]

    for lane_from, lane_to, column_from, column_to in jobs:
        rows = sum(stop - start for _, start, stop in spans[column_from:column_to])
        width = lane_to - lane_from if (lane_to - lane_from) * rows <= WHOLE else LANES

        def one_tile(step, carry, width=width, lane_from=lane_from, column_from=column_from, column_to=column_to):
            lanes = pl.ds(pl.multiple_of(lane_from + step * width, 128), width)
            query = query_ref[lanes, :]
            query_rank = query_rank_ref[:, lanes]
            best = jnp.broadcast_to(best_ref[:, lanes], (8, width))
            for column_ref, start, stop in spans[column_from:column_to]:
                best = fold(best, query, query_rank, column_ref, spread_ref[start:stop, :])
            best_ref[:, lanes] = jnp.max(best, axis=0, keepdims=True)
            return carry

        lax.fori_loop(0, (lane_to - lane_from) // width, one_tile, 0)
    if split:
        for place, out_ref in enumerate(out_refs):
            out_ref[...] = best_ref[:, place * tile : place * tile + tile]
    else:
        out_refs[0][...] = best_ref[...]


def columns_of(block):
    first, out = 0, []
    for piece in block:
        out.append((block[0], piece, first))
        first += piece.shape[0]
    return out


def compare(tile, columns, jobs, queries=(), held=(), best=None, over=None, keep=False, split=False):
    pieces = []

    def index_of(array):
        for place, other in enumerate(pieces):
            if other is array:
                return place
        pieces.append(array)
        return len(pieces) - 1

    column_plan = tuple((index_of(head), index_of(piece), offset) for head, piece, offset in columns)
    query_plan = tuple(tuple(index_of(piece) for piece in block) for block in queries)
    lane_count = held[0].shape[0] if held else len(queries) * tile
    width = pieces[0].shape[1]
    plan = (
        tile, query_plan, column_plan, tuple(jobs), bool(held), best is not None, over is not None, keep, split,
        len(pieces), lane_count,
    )
    operands = pieces + list(held) + [array for array in (best, over) if array is not None]
    query_shapes = [((lane_count, width), jnp.bfloat16), ((1, lane_count), jnp.float32)]
    lines = lane_count // tile if split else 1
    outs = [jax.ShapeDtypeStruct((1, lane_count // lines), jnp.float32)] * lines
    outs.append(jax.ShapeDtypeStruct((1, 128), jnp.int32))
    scratch = []
    if keep:
        outs += [jax.ShapeDtypeStruct(*shape) for shape in query_shapes]
    elif not held:
        scratch += [pltpu.VMEM(*shape) for shape in query_shapes]
    column_rows = sum(piece.shape[0] for _, piece, _ in columns)
    scratch += [pltpu.VMEM((column_rows, 128), jnp.float32), pltpu.VMEM((1, lane_count), jnp.float32)]
    vmem = pl.BlockSpec(memory_space=pltpu.VMEM)
    results = pl.pallas_call(
        functools.partial(compare_kernel, plan),
        out_shape=outs,
        in_specs=[vmem] * len(operands),
        out_specs=[vmem] * len(outs),
        scratch_shapes=scratch,
        compiler_params=pltpu.CompilerParams(vmem_limit_bytes=VMEM_LIMIT),
        name="compare",
    )(*operands)
    found = results[:lines] if split else results[0]
    return found, results[lines], results[lines + 1 :]


def place_kernel(chunks, tile, key_ref, *refs):
    keys = key_ref[...]
    out_ref = refs[-1]
    gathered = jnp.zeros((16, keys.shape[1]), jnp.float32)
    line = lax.broadcasted_iota(jnp.int32, (16, tile), 0)
    for chunk in range(chunks):
        value = refs[chunks - 1 - chunk][...]
        first = value.astype(jnp.bfloat16).astype(jnp.float32)
        second = (value - first).astype(jnp.bfloat16).astype(jnp.float32)
        third = value - first - second
        parts = jnp.where(line == 0, first, jnp.where(line == 1, second, jnp.where(line == 2, third, 0.0)))
        gathered += jnp.dot(
            parts.astype(jnp.bfloat16), one_hot(keys, chunk * tile, tile), preferred_element_type=jnp.float32
        )
    found = jnp.sum(gathered, axis=0, keepdims=True)
    if len(refs) > chunks + 1:
        over_ref, roomy_ref = refs[chunks : chunks + 2]
        found = jnp.where(over_ref[:, :1] > 0, roomy_ref[...], found)
    out_ref[...] = found


def place(chunks, tile, keys, values, *instead):
    vmem = pl.BlockSpec(memory_space=pltpu.VMEM)
    return pl.pallas_call(
        functools.partial(place_kernel, chunks, tile),
        out_shape=jax.ShapeDtypeStruct(keys.shape, jnp.float32),
        in_specs=[vmem] * (chunks + 1 + len(instead)),
        out_specs=vmem,
        compiler_params=pltpu.CompilerParams(vmem_limit_bytes=VMEM_LIMIT),
        name="place",
    )(keys, *reversed(values), *instead)


def swap(block, mask):
    return [from_partner(piece, "owners", mask) for piece in block]


def after(value, *others):
    return lax.optimization_barrier((value, *others))[0]


def give_back(chunks, tile, keys, best, *instead):
    returned = [best[0]] + [from_partner(best[k], "owners", SHARDS * k) for k in range(1, chunks)]
    return place(chunks, tile, keys, returned, *instead).reshape(keys.shape[1])


def roomy(chunks, tile, embeddings, buckets, ranks, home):
    sent, keys = route(((tile,),) * chunks, embeddings, buckets, ranks, home)
    own = [sent[0]] + [swap(sent[k], SHARDS * k) for k in range(1, chunks)]
    pair = own + [swap(block, 1) for block in own]
    lanes = chunks * tile
    columns = sum(map(columns_of, pair), [])
    best, over, held = compare(tile, columns, ((0, lanes, 0, len(columns)),), own, keep=True)
    columns = sum((columns_of(swap(block, 2)) for block in pair), [])
    best, *_ = compare(tile, columns, ((0, lanes, 0, len(columns)),), held=held, best=best, split=True)
    return give_back(chunks, tile, keys, best)


def snug(chunks, tile, embeddings, buckets, ranks, home):
    sent, keys = route(((tile,),) * chunks, embeddings, buckets, ranks, home)
    lanes, wave = chunks * tile, chunks // 4
    first_lanes = 3 * wave * tile // LANES * LANES

    def hop(blocks, mask, *others):
        return [swap([after(piece, *others) for piece in block] if others else block, mask) for block in blocks]

    def z_hop(place, *others):
        group = range(place * wave, place * wave + wave)
        return sum((hop(sent[k : k + 1], SHARDS * k, *others) if k else sent[:1] for k in group), [])

    def columns(*groups):
        return sum(map(columns_of, sum(groups, [])), [])

    z0 = z_hop(0)
    z1 = z_hop(1)
    z2 = z_hop(2)
    z3 = z_hop(3)
    y0 = hop(z0, 2)
    c0 = hop(z0, 1, z1[0][0])
    d0 = hop(y0, 1)
    y1 = hop(z1, 2)
    y2 = hop(z2, 2)
    seen = columns(z0, z1, z2, y0, c0, d0)
    k1, over, _ = compare(tile, seen, ((0, first_lanes, 0, len(seen)),), z0 + z1 + z2)
    c1 = hop(z1, 1, z1[0][0])
    c2 = hop(z2, 1, z2[0][0])
    d1 = hop(y1, 1, k1)
    z3 = [[after(piece, k1) for piece in block] for block in z3]
    y3 = hop(z3, 2)
    c3 = hop(z3, 1)
    d2 = hop(y2, 1)
    every = seen + columns(z3, y2, c3, d2, c1, c2, y1, d1)
    jobs = ((first_lanes, lanes, 0, len(seen)), (0, lanes, len(seen), len(every)))
    k2, over, held = compare(tile, every, jobs, z0 + z1 + z2 + z3, best=k1, over=over, keep=True)
    y3 = [[after(piece, k2) for piece in block] for block in y3]
    d3 = hop(y3, 1)
    late = columns(y3)
    k3, over, _ = compare(tile, late, ((0, lanes, 0, len(late)),), held=held, best=k2, over=over)
    last = columns(d3)
    best, over, _ = compare(tile, last, ((0, lanes, 0, len(last)),), held=held, best=k3, over=over, split=True)
    return keys, best, over


def body(embeddings, buckets, ranks):
    chunks = lax.axis_size("owners") // SHARDS
    full = SHARDS * 2 * embeddings.shape[0] // lax.axis_size("owners")
    tile = -(-(3 * full // 4) // 128) * 128
    roomy_tile = -(-(full + EXTRA) // 128) * 128
    home = (lax.axis_index("owners") // SHARDS).astype(jnp.int32).reshape(1)
    operands = (embeddings, buckets, ranks, home)
    keys, best, over = snug(chunks, tile, *operands)
    other = lax.cond(
        over[0, 0] > 0,
        functools.partial(roomy, chunks, roomy_tile),
        lambda embeddings, *_: jnp.zeros((embeddings.shape[0],), jnp.float32),
        *operands,
    )
    return give_back(chunks, tile, keys, best, over, other.reshape(keys.shape))


def solution(mesh):
    in_specs = (P(("groups", "owners"), None), P(("groups", "owners")), P(("groups", "owners")))
    out_specs = P(("groups", "owners"))
    return jax.shard_map(body, mesh=mesh, in_specs=in_specs, out_specs=out_specs, check_vma=False)
```
